256 devices in a mesh: depth: 8 (over y_lo, x), row: 4 (over y_hi, core), col: 8 (over z).
Axes of the slice: x: 4, y: 4 (y_hi: 2, y_lo: 2; y = y_hi * 2 + y_lo), z: 8, core: 2. Of those that a mesh axis runs over, the one named last changes fastest.
Arguments:
- tokens: bfloat16 [4096, 3072], P('depth', 'row'), may hold values from -6 to 6
- gate_weight: bfloat16 [3072, 16384], P('row', 'col'), may hold values from -0.109375 to 0.109375
- up_weight: bfloat16 [3072, 16384], P('row', 'col'), may hold values from -0.109375 to 0.109375
- down_weight: bfloat16 [16384, 3072], P('col', 'row'), may hold values from -0.046875 to 0.046875
- output_grad: bfloat16 [4096, 3072], P('depth', 'row'), may hold values from -6 to 6
Outputs:
- mlp_output: bfloat16 [4096, 3072], P('depth', 'row')
- input_grad: bfloat16 [4096, 3072], P('depth', 'row')
- gate_weight_grad: float32 [8, 3072, 2048], P('depth', 'row', 'col')
- up_weight_grad: float32 [8, 3072, 2048], P('depth', 'row', 'col')
- down_weight_grad: float32 [8, 2048, 3072], P('depth', 'col', 'row')
The draws below stay inside these ranges and needn't reach their ends.
All inputs are finite; a program needn't handle non-finite values.
Results may differ from the reference program's by a relative error of at most 0.005.
Values may be sent and summed in bfloat16 or wider, within the bound.
No kernel may reach another device: no remote copies, remote signals or barrier semaphores. Data moves between devices by JAX's collectives and lax.ppermute only.
A program may use at most 128 MiB of HBM per device.

```python
import jax
import jax.numpy as jnp

D = 3072
FF = 16384
TOKENS = 4096
N_DEPTH = 8
N_COL = 8


def level_of(key, shape, cuts, smallest, top_value):
    gain, own = 1.0, jax.random.fold_in(key, 6)
    for position, shards_of in cuts:
        draws = jnp.exp(jax.random.uniform(jax.random.fold_in(own, position), (shards_of,), jnp.float32, smallest / len(cuts), top_value / len(cuts)))
        gain = gain * jnp.repeat(draws, shape[position] // shards_of).reshape([-1 if axis == position else 1 for axis in range(len(shape))])
    return gain


def bell_draw(key, shape, spread, bound, shards=(), held_as=jnp.bfloat16):
    gain = level_of(key, shape, shards, -0.22, 0.18) if shards else 1.0
    entries = jax.random.normal(key, shape, jnp.float32) * spread * gain
    return jnp.minimum(jnp.maximum(entries, -bound), bound).astype(held_as)


def setup_inputs(seed: int = 0) -> dict:
    streams_of = jax.random.split(jax.random.key(seed), 6)
    tokens = bell_draw(streams_of[0], (TOKENS, D), 1.0, 6.0, ((0, 8), (1, 4)))
    gate_weight = bell_draw(streams_of[1], (D, FF), D ** -0.5, 0.109375, ((0, 4), (1, 8)))
    up_weight = bell_draw(streams_of[2], (D, FF), D ** -0.5, 0.109375, ((0, 4), (1, 8)))
    down_weight = bell_draw(streams_of[3], (FF, D), FF ** -0.5, 0.046875, ((0, 8), (1, 4)))
    output_grad = bell_draw(streams_of[4], (TOKENS, D), 1.0, 6.0, ((0, 8), (1, 4)))
    return dict(tokens=tokens, gate_weight=gate_weight, up_weight=up_weight, down_weight=down_weight, output_grad=output_grad)


def reference(tokens, gate_weight, up_weight, down_weight, output_grad):
    gate_values = jnp.dot(tokens, gate_weight, preferred_element_type=jnp.float32)
    up_values = jnp.dot(tokens, up_weight, preferred_element_type=jnp.float32)
    sigmoid_values = jax.nn.sigmoid(gate_values)
    silu_values = gate_values * sigmoid_values
    hidden = (silu_values * up_values).astype(jnp.bfloat16)
    mlp_output = jnp.dot(hidden, down_weight, preferred_element_type=jnp.float32).astype(jnp.bfloat16)
    hidden_grad = jnp.dot(output_grad, down_weight.T, preferred_element_type=jnp.float32)
    gate_grad = (hidden_grad * up_values * sigmoid_values * (1.0 + gate_values * (1.0 - sigmoid_values))).astype(jnp.bfloat16)
    up_grad = (hidden_grad * silu_values).astype(jnp.bfloat16)
    input_grad = (jnp.dot(gate_grad, gate_weight.T, preferred_element_type=jnp.float32)
                  + jnp.dot(up_grad, up_weight.T, preferred_element_type=jnp.float32)).astype(jnp.bfloat16)
    full_gate = jnp.dot(tokens.T, gate_grad, preferred_element_type=jnp.float32) * 0.03125
    full_up = jnp.dot(tokens.T, up_grad, preferred_element_type=jnp.float32) * 0.03125
    full_down = jnp.dot(hidden.T, output_grad, preferred_element_type=jnp.float32) * 0.03125
    sub_width = FF // (N_COL * N_DEPTH)
    gate_weight_grad = full_gate.reshape(D, N_COL, N_DEPTH, sub_width).transpose(2, 0, 1, 3).reshape(N_DEPTH, D, FF // N_DEPTH)
    up_weight_grad = full_up.reshape(D, N_COL, N_DEPTH, sub_width).transpose(2, 0, 1, 3).reshape(N_DEPTH, D, FF // N_DEPTH)
    down_weight_grad = full_down.reshape(N_COL, N_DEPTH, sub_width, D).transpose(1, 0, 2, 3).reshape(N_DEPTH, FF // N_DEPTH, D)
    return (mlp_output, input_grad, gate_weight_grad, up_weight_grad, down_weight_grad)
```

```python
import functools

import jax
import jax.numpy as jnp
from jax import lax
from jax.experimental import pallas as pl
from jax.experimental.pallas import tpu as pltpu
from jax.sharding import PartitionSpec as P

grad_scale = 0.03125
wide = 256
n_x = 4
n_col = 8
mib = 1024 * 1024
bf16 = jnp.bfloat16
f32 = jnp.float32

core_swap = [(0, 1), (1, 0), (2, 3), (3, 2)]
half_swap = [(0, 2), (2, 0), (1, 3), (3, 1)]


def x_shift(step):
    return [(y * n_x + x, y * n_x + (x + step) % n_x) for y in range(2) for x in range(n_x)]


def home_swaps():
    first, second = [], []
    for y in range(2):
        for x in range(n_x):
            for half in range(2):
                for core in range(2):
                    at = lambda y_to, core_to: (y_to * n_x + x) * 4 + half * 2 + core_to
                    if core == y:
                        first.append((at(y, core), at(y, 1 - core)))
                    else:
                        first.append((at(y, core), at(1 - y, core)))
                        second.append((at(y, core), at(1 - y, 1 - core)))
    return first, second


home_first, home_second = home_swaps()


def params(limit):
    return pltpu.CompilerParams(vmem_limit_bytes=limit * mib)


def cost(time):
    return pl.CostEstimate(flops=1, bytes_accessed=int(time * 1 * 3.3e6), transcendentals=0)


def mm(left, right):
    return jnp.dot(left, right, preferred_element_type=f32)


def mm_t(left, right):
    return lax.dot_general(left, right, (((1,), (1,)), ((), ())), preferred_element_type=f32)


def after(value, *others):
    return lax.optimization_barrier((value,) + others)[0]


class Chain:
    def __init__(self):
        self.last = None

    def __call__(self, fn, *args):
        if self.last is not None:
            args = (after(args[0], self.last),) + args[1:]
        out = fn(*args)
        self.last = out[0] if isinstance(out, (tuple, list)) else out
        return out


def own_block(step, spot):
    return spot[1] * n_x + lax.rem(spot[0] + step, n_x)


def oth_block(step, spot):
    return lax.rem(spot[0] + step, n_x)


def gate_up_body(spot, own_ref, oth_ref, gate_ref, up_ref, oth_gate_ref, oth_up_ref, out_ref, send_ref):
    for k, (w, oth_w) in enumerate(((gate_ref, oth_gate_ref), (up_ref, oth_up_ref))):
        value = mm(own_ref[...], w[...]) + mm(oth_ref[...], oth_w[...])
        out_ref[:, k * wide : (k + 1) * wide] = value
        send_ref[:, k * wide : (k + 1) * wide] = value.astype(bf16)


def gate_up_partial(steps, spot, own, oth, gate_weight, up_weight, oth_gate, oth_up):
    rows, feat = own.shape
    n = len(steps)
    part = pl.BlockSpec((rows // 2, feat), lambda j, i, s: (i, 0))
    own_w = pl.BlockSpec((feat, wide), lambda j, i, s: (0, own_block(steps[0] + 2 * j, s)))
    oth_w = pl.BlockSpec((feat, wide), lambda j, i, s: (0, oth_block(steps[0] + 2 * j, s)))
    out = pl.BlockSpec((rows // 2, 2 * wide), lambda j, i, s: (i, j))
    return pl.pallas_call(
        gate_up_body,
        grid_spec=pltpu.PrefetchScalarGridSpec(
            num_scalar_prefetch=1,
            grid=(n, 2),
            in_specs=[part, part, own_w, own_w, oth_w, oth_w],
            out_specs=[out, out],
        ),
        out_shape=[
            jax.ShapeDtypeStruct((rows, 2 * wide * n), f32),
            jax.ShapeDtypeStruct((rows, 2 * wide * n), bf16),
        ],
        compiler_params=params(56),
        cost_estimate=cost(4.5),
        name="gate_up_partial",
    )(spot, own, oth, gate_weight, up_weight, oth_gate, oth_up)


def joint_body(gate_up_step, hg_steps, spot, *refs):
    refs = list(refs)
    send_ref, outs = refs[-1], []
    at = 0
    if gate_up_step is not None:
        own_ref, oth_ref, gate_ref, up_ref, oth_gate_ref, oth_up_ref = refs[:6]
        refs = refs[6:]
        out_ref = refs[-2] if not hg_steps else refs[-3]
        for k, (w, oth_w) in enumerate(((gate_ref, oth_gate_ref), (up_ref, oth_up_ref))):
            value = mm(own_ref[...], w[...]) + mm(oth_ref[...], oth_w[...])
            out_ref[:, k * wide : (k + 1) * wide] = value
            send_ref[:, k * wide : (k + 1) * wide] = value.astype(bf16)
        at = 2 * wide
    own_ref, oth_ref = refs[:2]
    out_ref = refs[-2]
    for k in range(len(hg_steps)):
        value = mm_t(own_ref[...], refs[2 + 2 * k][...]) + mm_t(oth_ref[...], refs[3 + 2 * k][...])
        out_ref[:, k * wide : (k + 1) * wide] = value
        send_ref[:, at + k * wide : at + (k + 1) * wide] = value.astype(bf16)


def joint_partial(gate_up_step, hg_steps, spot, tokens_pair, gate_up_weights, grad_pair, down_weights):
    rows, feat = grad_pair[0].shape
    whole = pl.BlockSpec((rows, feat), lambda j, s: (0, 0))
    operands, specs, shapes = [], [], []
    if gate_up_step is not None:
        operands += [*tokens_pair, *gate_up_weights]
        specs += [whole, whole]
        specs += [pl.BlockSpec((feat, wide), lambda j, s: (0, own_block(gate_up_step, s)))] * 2
        specs += [pl.BlockSpec((feat, wide), lambda j, s: (0, oth_block(gate_up_step, s)))] * 2
        shapes.append(jax.ShapeDtypeStruct((rows, 2 * wide), f32))
    operands += [*grad_pair]
    specs += [whole, whole]
    for step in hg_steps:
        operands += [*down_weights]
        specs.append(pl.BlockSpec((wide, feat), lambda j, s, step=step: (own_block(step, s), 0)))
        specs.append(pl.BlockSpec((wide, feat), lambda j, s, step=step: (oth_block(step, s), 0)))
    shapes.append(jax.ShapeDtypeStruct((rows, wide * len(hg_steps)), f32))
    total = sum(shape.shape[1] for shape in shapes)
    shapes.append(jax.ShapeDtypeStruct((rows, total), bf16))
    return pl.pallas_call(
        functools.partial(joint_body, gate_up_step, hg_steps),
        grid_spec=pltpu.PrefetchScalarGridSpec(
            num_scalar_prefetch=1,
            grid=(1,),
            in_specs=specs,
            out_specs=[pl.BlockSpec(shape.shape, lambda j, s: (0, 0)) for shape in shapes],
        ),
        out_shape=shapes,
        compiler_params=params(56),
        cost_estimate=cost(6),
        name="joint_partial",
    )(spot, *operands)


def hidden_body(part_ref, got_ref, hidden_ref, hidden_t_ref):
    gate_up = part_ref[...] + got_ref[...].astype(f32)
    gate_values = gate_up[:, :wide]
    up_values = gate_up[:, wide:]
    silu_values = gate_values * jax.nn.sigmoid(gate_values)
    hidden = (silu_values * up_values).astype(bf16)
    hidden_ref[...] = hidden
    hidden_t_ref[...] = hidden.T


def hidden_step(part, got):
    rows = part.shape[0]
    n = part.shape[1] // (2 * wide)
    pair = pl.BlockSpec((rows, 2 * wide), lambda j: (0, j))
    return pl.pallas_call(
        hidden_body,
        grid=(n,),
        in_specs=[pair, pair],
        out_specs=[
            pl.BlockSpec((rows, wide), lambda j: (0, j)),
            pl.BlockSpec((wide, rows), lambda j: (j, 0)),
        ],
        out_shape=[
            jax.ShapeDtypeStruct((rows, wide * n), bf16),
            jax.ShapeDtypeStruct((wide * n, rows), bf16),
        ],
        compiler_params=params(20),
        cost_estimate=cost(1),
        name="hidden_step",
    )(part, got)


def grads_body(part_ref, got_ref, hg_ref, hg_got_ref, grads_ref):
    gate_up = part_ref[...] + got_ref[...].astype(f32)
    hidden_grad = hg_ref[...] + hg_got_ref[...].astype(f32)
    gate_values = gate_up[:, :wide]
    up_values = gate_up[:, wide:]
    sigmoid_values = jax.nn.sigmoid(gate_values)
    silu_values = gate_values * sigmoid_values
    gate_grad = hidden_grad * up_values * sigmoid_values * (1.0 + gate_values * (1.0 - sigmoid_values))
    up_grad = hidden_grad * silu_values
    grads_ref[:, :wide] = gate_grad.astype(bf16)
    grads_ref[:, wide:] = up_grad.astype(bf16)


def grads_step(hg_at, got_at, part, got, hg, hg_got):
    rows = part.shape[0]
    n = part.shape[1] // (2 * wide)
    pair = pl.BlockSpec((rows, 2 * wide), lambda j: (0, j))
    return pl.pallas_call(
        grads_body,
        grid=(n,),
        in_specs=[
            pair,
            pair,
            pl.BlockSpec((rows, wide), lambda j: (0, hg_at + j)),
            pl.BlockSpec((rows, wide), lambda j: (0, got_at + j)),
        ],
        out_specs=pair,
        out_shape=jax.ShapeDtypeStruct((rows, 2 * wide * n), bf16),
        compiler_params=params(20),
        cost_estimate=cost(1.3),
        name="grads_step",
    )(part, got, hg, hg_got)


def mlp_body(spot, far_ref, near_ref, last_ref, w2, w1, w3, w0, out_ref):
    total = mm(far_ref[...], w2[...]) + mm(near_ref[:, :wide], w1[...])
    total += mm(near_ref[:, wide:], w3[...]) + mm(last_ref[...], w0[...])
    out_ref[...] = total.astype(out_ref.dtype)


def input_body(spot, far_ref, near_ref, last_ref, g2, g1, g3, g0, u2, u1, u3, u0, out_ref):
    total = mm_t(far_ref[:, :wide], g2[...]) + mm_t(far_ref[:, wide:], u2[...])
    total += mm_t(near_ref[:, :wide], g1[...]) + mm_t(near_ref[:, wide : 2 * wide], u1[...])
    total += mm_t(near_ref[:, 2 * wide : 3 * wide], g3[...]) + mm_t(near_ref[:, 3 * wide :], u3[...])
    total += mm_t(last_ref[:, :wide], g0[...]) + mm_t(last_ref[:, wide:], u0[...])
    out_ref[...] = total.astype(out_ref.dtype)


def activation_part(body, block_of, dtype, name, spot, values, weights, by_rows):
    rows = values[0].shape[0]
    feat = weights[0].shape[1 if by_rows else 0]
    whole = [pl.BlockSpec(v.shape, lambda j, s: (0, 0)) for v in values]
    blocks = []
    for _ in weights:
        for step in (2, 1, 3, 0):
            if by_rows:
                blocks.append(pl.BlockSpec((wide, wide), lambda j, s, step=step: (block_of(step, s), j)))
            else:
                blocks.append(pl.BlockSpec((wide, wide), lambda j, s, step=step: (j, block_of(step, s))))
    return pl.pallas_call(
        body,
        grid_spec=pltpu.PrefetchScalarGridSpec(
            num_scalar_prefetch=1,
            grid=(feat // wide,),
            in_specs=whole + blocks,
            out_specs=pl.BlockSpec((rows, wide), lambda j, s: (0, j)),
        ),
        out_shape=jax.ShapeDtypeStruct((rows, feat), dtype),
        compiler_params=params(20),
        cost_estimate=cost(2.5),
        name=name,
    )(spot, *values, *[w for w in weights for _ in range(4)])


def join_body(own_ref, got_ref, out_ref):
    out_ref[...] = (own_ref[...] + got_ref[...].astype(f32)).astype(out_ref.dtype)


def join(dtype, own, got):
    rows, feat = own.shape
    block = pl.BlockSpec((rows // 2, feat), lambda j: (j, 0))
    return pl.pallas_call(
        join_body,
        grid=(2,),
        in_specs=[block, block],
        out_specs=block,
        out_shape=jax.ShapeDtypeStruct(own.shape, dtype),
        compiler_params=params(20),
        cost_estimate=cost(1),
        name="join",
    )(own, got)


def far_body(a0, a1, b0, b1, *out_refs):
    pieces = len(out_refs) // 2
    for a, b, refs in ((a0, b0, out_refs[:pieces]), (a1, b1, out_refs[pieces:])):
        value = mm(a[...], b[...]).astype(bf16)
        n = value.shape[1] // pieces
        for k, ref in enumerate(refs):
            ref[...] = value[:, k * n : (k + 1) * n]


def far_terms(pieces, a, b):
    m, n = a[0].shape[0], b[0].shape[1]
    return pl.pallas_call(
        far_body,
        out_shape=[jax.ShapeDtypeStruct((m, n // pieces), bf16)] * (2 * pieces),
        compiler_params=params(20),
        cost_estimate=cost(1),
        name="far_terms",
    )(*a, *b)


def near_body(a0, a1, c0, c1, b0, b1, d0, d1, *refs):
    pieces = len(refs) // 2 - 1
    rights, lefts = refs[:pieces], refs[pieces : 2 * pieces]
    right_ref, left_ref = refs[-2:]
    m, n = rights[0].shape

    def add(value, got_refs, out_ref, at):
        for k, got in enumerate(got_refs):
            some = value[:, k * n : (k + 1) * n] + got[...].astype(f32)
            out_ref[at : at + m, k * n : (k + 1) * n] = some.astype(bf16)

    add(mm(a0[...], b0[...]), rights, right_ref, 0)
    right_ref[m:, :] = mm(a1[...], b1[...]).astype(bf16)
    left_ref[:m, :] = mm(c0[...], d0[...]).astype(bf16)
    add(mm(c1[...], d1[...]), lefts, left_ref, m)


def window(shape, at):
    return pl.BlockSpec(shape, lambda i: at)


def near_terms(operands, specs, m, n):
    shape = jax.ShapeDtypeStruct((2 * m, n), bf16)
    inner = operands[0].shape[1]
    return pl.pallas_call(
        near_body,
        grid=(1,),
        in_specs=specs,
        out_specs=[window(shape.shape, (0, 0))] * 2,
        out_shape=[shape, shape],
        compiler_params=params(20),
        cost_estimate=cost(2.2),
        name="near_terms",
    )(*operands)


def last_body(spot, a0, a1, b0, b1, from_left, from_right, keep_ref, first_ref, second_ref):
    m = keep_ref.shape[0]
    own = mm(a0[...], b0[...]) + from_left[:m, :].astype(f32) + from_right[:m, :].astype(f32)
    oth = mm(a1[...], b1[...]) + from_left[m:, :].astype(f32) + from_right[m:, :].astype(f32)
    keep_ref[...] = own
    second_ref[...] = oth.astype(bf16)

    @pl.when(spot[3] == 1)
    def _():
        first_ref[...] = oth.astype(bf16)

    @pl.when(spot[3] == 0)
    def _():
        first_ref[...] = own.astype(bf16)


def last_terms(spot, operands, specs, m, n):
    inner = operands[0].shape[1]
    block = pl.BlockSpec((m, n), lambda i, s: (0, 0))
    return pl.pallas_call(
        last_body,
        grid_spec=pltpu.PrefetchScalarGridSpec(
            num_scalar_prefetch=1,
            grid=(1,),
            in_specs=[pl.BlockSpec(shape, lambda i, s, at=at: at) for shape, at in specs],
            out_specs=[block, block, block],
        ),
        out_shape=[
            jax.ShapeDtypeStruct((m, n), f32),
            jax.ShapeDtypeStruct((m, n), bf16),
            jax.ShapeDtypeStruct((m, n), bf16),
        ],
        compiler_params=params(20),
        cost_estimate=cost(1.3),
        name="last_terms",
    )(spot, *operands)


def collect_body(mlp_ref, parts_ref, out_ref):
    height, feat = mlp_ref.shape
    total = parts_ref[:height, :].astype(f32)
    for j in range(1, n_col):
        total = total + parts_ref[j * height : (j + 1) * height, :].astype(f32)
    out_ref[:, :feat] = mlp_ref[...].astype(bf16)
    out_ref[:, feat:] = total.astype(bf16)


def collect(mlp_sum, parts):
    height, feat = mlp_sum.shape
    return pl.pallas_call(
        collect_body,
        out_shape=jax.ShapeDtypeStruct((height, 2 * feat), bf16),
        compiler_params=params(20),
        cost_estimate=cost(1),
        name="collect",
    )(mlp_sum, parts)


def finish_body(spot, one_ref, keep_ref, two_ref, *out_refs):
    one = one_ref[...].astype(f32)
    n = out_refs[0].shape[2]

    def store(value):
        for k, out_ref in enumerate(out_refs):
            out_ref[0] = value[:, k * n : (k + 1) * n]

    @pl.when(spot[3] == 1)
    def _():
        store((keep_ref[...] + one) * grad_scale)

    @pl.when(spot[3] == 0)
    def _():
        store((two_ref[...].astype(f32) + one) * grad_scale)


def finish(outs, spot, one, keep, two):
    m, n = one.shape
    block = pl.BlockSpec((m, n), lambda i, s: (0, 0))
    shape = jax.ShapeDtypeStruct((1, m, n // outs), f32)
    return pl.pallas_call(
        finish_body,
        grid_spec=pltpu.PrefetchScalarGridSpec(
            num_scalar_prefetch=1,
            grid=(1,),
            in_specs=[block] * 3,
            out_specs=[pl.BlockSpec(shape.shape, lambda i, s: (0, 0, 0))] * outs,
        ),
        out_shape=[shape] * outs,
        compiler_params=params(20),
        cost_estimate=cost(1.5),
        name="finish",
    )(spot, one, keep, two)


def local(tokens, gate_weight, up_weight, down_weight, output_grad):
    rows, feat = tokens.shape
    depth_id = lax.axis_index("depth")
    x_id = depth_id % n_x
    y_lo = depth_id // n_x
    core = lax.axis_index("row") % 2
    home = core == y_lo
    spot = jnp.stack([x_id, core, lax.axis_index("col"), home.astype(jnp.int32)]).astype(jnp.int32)
    run = Chain()

    swap = lambda value: lax.ppermute(value, "row", core_swap)
    cross = lambda value: lax.ppermute(value, "row", half_swap)
    right = lambda value: lax.ppermute(value, "depth", x_shift(1))
    left = lambda value: lax.ppermute(value, "depth", x_shift(-1))
    home_one = lambda value: lax.ppermute(value, ("depth", "row"), home_first)
    home_two = lambda value: lax.ppermute(value, ("depth", "row"), home_second)
    trade = lambda value: lax.all_to_all(value, "col", 0, 0, tiled=True)

    half = gate_weight.shape[1] // 2
    far, near, last = (2,), (1, 3), (0,)
    oth_columns = lambda value: lax.dynamic_slice_in_dim(value, (1 - core) * half, half, 1)
    oth_rows = lambda value: lax.dynamic_slice_in_dim(value, (1 - core) * half, half, 0)

    tokens_oth = swap(tokens)
    output_grad_oth = swap(output_grad)
    grad_halves = [output_grad, output_grad_oth]
    gate_oth = swap(run(oth_columns, gate_weight))
    up_oth = swap(run(oth_columns, after(up_weight, tokens_oth)))
    gate_up_of = lambda steps: run(
        functools.partial(gate_up_partial, steps),
        spot, tokens, tokens_oth, gate_weight, up_weight, gate_oth, up_oth,
    )
    part_far, send = gate_up_of(far)
    got_far = cross(send)
    down_oth = swap(run(oth_rows, down_weight))
    part_near, send = gate_up_of(near)
    got_near = cross(after(send, got_far))

    hidden_far, hidden_t = run(hidden_step, part_far, got_far)
    down_far = run(lambda a, b0, b1: far_terms(1, (a, a), (b0, b1)), hidden_t, *grad_halves)
    down_far = (right(down_far[0]), left(down_far[1]))
    joint = lambda gate_up_step, hg_steps: run(
        functools.partial(joint_partial, gate_up_step, hg_steps),
        spot,
        (tokens, tokens_oth),
        (gate_weight, up_weight, gate_oth, up_oth),
        grad_halves,
        (down_weight, down_oth),
    )
    part_last, hg_far, send = joint(last[0], far)
    got_last = cross(after(send, got_near))

    hidden_near, hidden_t = run(hidden_step, part_near, got_near)
    t_spec = [window((wide, rows), (0, 0))] * 2 + [window((wide, rows), (1, 0))] * 2
    o_spec = [window((rows, feat), (0, 0))] * 4
    f_spec = [window((wide, feat), (0, 0))] * 2
    down_near = run(
        lambda a, b0, b1, r, l: near_terms(
            (a, a, a, a, b0, b1, b0, b1, r, l), t_spec + o_spec + f_spec, wide, feat
        ),
        hidden_t, *grad_halves, *down_far,
    )
    down_near = (right(down_near[0]), left(down_near[1]))
    hg_rest, send = joint(None, near + last)
    hg_got = cross(after(send, got_last))
    tokens_t = [run(jnp.transpose, value) for value in (tokens, tokens_oth)]

    grads_far = run(functools.partial(grads_step, 0, 2), part_far, got_far, hg_far, got_last)
    gate_up_far = run(lambda b, a0, a1: far_terms(1, (a0, a1), (b, b)), grads_far, *tokens_t)
    gate_up_far = (right(gate_up_far[0]), left(gate_up_far[1]))
    hidden_last, hidden_t = run(hidden_step, part_last, got_last)
    down_spec = (
        [((wide, rows), (0, 0))] * 2 + [((rows, feat), (0, 0))] * 2 + [((2 * wide, feat), (0, 0))] * 2
    )
    down_keep, first, second = run(
        lambda s, a, b0, b1, l, r: last_terms(s, (a, a, b0, b1, l, r), down_spec, wide, feat),
        spot, hidden_t, *grad_halves, *down_near,
    )
    down_first, down_second = home_one(first), home_two(second)
    hidden = (hidden_far, hidden_near, hidden_last)
    mlp_of = lambda block_of, dtype, weight: run(
        lambda s, w, *v: activation_part(mlp_body, block_of, dtype, "mlp_part", s, v, [w], True),
        spot, weight, *hidden,
    )
    mlp_oth = swap(mlp_of(oth_block, bf16, down_oth))
    mlp_own = mlp_of(own_block, f32, down_weight)
    grads_near = run(functools.partial(grads_step, 0, 0), part_near, got_near, hg_rest, hg_got)
    grads_last = run(functools.partial(grads_step, 2, 2), part_last, got_last, hg_rest, hg_got)
    grads = (grads_far, grads_near, grads_last)
    two = 2 * wide
    specs = [window((feat, rows), (0, 0))] * 4
    specs += [window((rows, two), (0, 0))] * 2 + [window((rows, two), (0, 1))] * 2
    specs += [window((feat, two), (0, 0))] * 2
    gate_up_near = run(
        lambda b, a0, a1, *got: near_terms((a0, a1, a0, a1, b, b, b, b, *got), specs, feat, two),
        grads_near, *tokens_t, *gate_up_far,
    )
    gate_up_near = (right(gate_up_near[0]), left(gate_up_near[1]))
    mlp_sum = lax.psum_scatter(
        run(functools.partial(join, f32), mlp_own, mlp_oth), "col", scatter_dimension=0, tiled=True
    )
    input_of = lambda block_of, dtype, *weights: run(
        lambda s, g, u, *v: activation_part(input_body, block_of, dtype, "input_part", s, v, [g, u], False),
        spot, *weights, *grads,
    )
    input_oth = swap(input_of(oth_block, bf16, gate_oth, up_oth))
    input_own = input_of(own_block, f32, gate_weight, up_weight)
    input_parts = trade(run(functools.partial(join, bf16), input_own, input_oth))

    (down_out,) = run(functools.partial(finish, 1), spot, down_first, down_keep, down_second)
    end_spec = [((feat, rows), (0, 0))] * 2 + [((rows, two), (0, 0))] * 2 + [((2 * feat, two), (0, 0))] * 2
    gate_up_keep, first, second = run(
        lambda s, a0, a1, b, l, r: last_terms(s, (a0, a1, b, b, l, r), end_spec, feat, two),
        spot, *tokens_t, grads_last, *gate_up_near,
    )
    gate_up_first, gate_up_second = home_one(first), home_two(second)
    both = lax.all_gather(run(collect, mlp_sum, input_parts), "col", axis=0, tiled=True)
    mlp_output, input_grad = both[:, :feat], both[:, feat:]
    gate_out, up_out = run(functools.partial(finish, 2), spot, gate_up_first, gate_up_keep, gate_up_second)
    return (mlp_output, input_grad, gate_out, up_out, down_out)


def solution(mesh):
    placed = (
        P("depth", "row"),
        P("row", "col"),
        P("row", "col"),
        P("col", "row"),
        P("depth", "row"),
    )
    return jax.shard_map(
        local,
        mesh=mesh,
        in_specs=placed,
        out_specs=(
            P("depth", "row"),
            P("depth", "row"),
            P("depth", "row", "col"),
            P("depth", "row", "col"),
            P("depth", "col", "row"),
        ),
        check_vma=False,
    )
```

```python
import functools

import jax
import jax.numpy as jnp
from jax import lax
from jax.experimental import pallas as pl
from jax.experimental.pallas import tpu as pltpu
from jax.sharding import PartitionSpec as P

grad_scale = 0.03125
wide = 256
n_x = 4
n_col = 8
mib = 1024 * 1024
bf16 = jnp.bfloat16
f32 = jnp.float32

core_swap = [(0, 1), (1, 0), (2, 3), (3, 2)]
half_swap = [(0, 2), (2, 0), (1, 3), (3, 1)]


def x_shift(step):
    return [(y * n_x + x, y * n_x + (x + step) % n_x) for y in range(2) for x in range(n_x)]


def home_swaps():
    first, second = [], []
    for y in range(2):
        for x in range(n_x):
            for half in range(2):
                for core in range(2):
                    at = lambda y_to, core_to: (y_to * n_x + x) * 4 + half * 2 + core_to
                    if core == y:
                        first.append((at(y, core), at(y, 1 - core)))
                    else:
                        first.append((at(y, core), at(1 - y, core)))
                        second.append((at(y, core), at(1 - y, 1 - core)))
    return first, second


home_first, home_second = home_swaps()


def params(limit):
    return pltpu.CompilerParams(vmem_limit_bytes=limit * mib)


def cost(time):
    return pl.CostEstimate(flops=1, bytes_accessed=int(time * 1 * 3.3e6), transcendentals=0)


def mm(left, right):
    return jnp.dot(left, right, preferred_element_type=f32)


def mm_t(left, right):
    return lax.dot_general(left, right, (((1,), (1,)), ((), ())), preferred_element_type=f32)


def after(value, *others):
    return lax.optimization_barrier((value,) + others)[0]


class Chain:
    def __init__(self):
        self.last = None

    def __call__(self, fn, *args):
        if self.last is not None:
            args = (after(args[0], self.last),) + args[1:]
        out = fn(*args)
        self.last = out[0] if isinstance(out, (tuple, list)) else out
        return out


def own_block(step, spot):
    return spot[1] * n_x + lax.rem(spot[0] + step, n_x)


def oth_block(step, spot):
    return lax.rem(spot[0] + step, n_x)


def gate_up_body(spot, own_ref, oth_ref, gate_ref, up_ref, oth_gate_ref, oth_up_ref, out_ref, send_ref):
    for k, (w, oth_w) in enumerate(((gate_ref, oth_gate_ref), (up_ref, oth_up_ref))):
        value = mm(own_ref[...], w[...]) + mm(oth_ref[...], oth_w[...])
        out_ref[:, k * wide : (k + 1) * wide] = value
        send_ref[:, k * wide : (k + 1) * wide] = value.astype(bf16)


def gate_up_partial(steps, spot, own, oth, gate_weight, up_weight, oth_gate, oth_up):
    rows, feat = own.shape
    n = len(steps)
    part = pl.BlockSpec((rows // 2, feat), lambda j, i, s: (i, 0))
    own_w = pl.BlockSpec((feat, wide), lambda j, i, s: (0, own_block(steps[0] + 2 * j, s)))
    oth_w = pl.BlockSpec((feat, wide), lambda j, i, s: (0, oth_block(steps[0] + 2 * j, s)))
    out = pl.BlockSpec((rows // 2, 2 * wide), lambda j, i, s: (i, j))
    return pl.pallas_call(
        gate_up_body,
        grid_spec=pltpu.PrefetchScalarGridSpec(
            num_scalar_prefetch=1,
            grid=(n, 2),
            in_specs=[part, part, own_w, own_w, oth_w, oth_w],
            out_specs=[out, out],
        ),
        out_shape=[
            jax.ShapeDtypeStruct((rows, 2 * wide * n), f32),
            jax.ShapeDtypeStruct((rows, 2 * wide * n), bf16),
        ],
        compiler_params=params(56),
        cost_estimate=cost(4.5),
        name="gate_up_partial",
    )(spot, own, oth, gate_weight, up_weight, oth_gate, oth_up)


def joint_body(gate_up_step, hg_steps, spot, *refs):
    refs = list(refs)
    send_ref, outs = refs[-1], []
    at = 0
    if gate_up_step is not None:
        own_ref, oth_ref, gate_ref, up_ref, oth_gate_ref, oth_up_ref = refs[:6]
        refs = refs[6:]
        out_ref = refs[-2] if not hg_steps else refs[-3]
        for k, (w, oth_w) in enumerate(((gate_ref, oth_gate_ref), (up_ref, oth_up_ref))):
            value = mm(own_ref[...], w[...]) + mm(oth_ref[...], oth_w[...])
            out_ref[:, k * wide : (k + 1) * wide] = value
            send_ref[:, k * wide : (k + 1) * wide] = value.astype(bf16)
        at = 2 * wide
    own_ref, oth_ref = refs[:2]
    out_ref = refs[-2]
    for k in range(len(hg_steps)):
        value = mm_t(own_ref[...], refs[2 + 2 * k][...]) + mm_t(oth_ref[...], refs[3 + 2 * k][...])
        out_ref[:, k * wide : (k + 1) * wide] = value
        send_ref[:, at + k * wide : at + (k + 1) * wide] = value.astype(bf16)


def joint_partial(gate_up_step, hg_steps, spot, tokens_pair, gate_up_weights, grad_pair, down_weights):
    rows, feat = grad_pair[0].shape
    whole = pl.BlockSpec((rows, feat), lambda j, s: (0, 0))
    operands, specs, shapes = [], [], []
    if gate_up_step is not None:
        operands += [*tokens_pair, *gate_up_weights]
        specs += [whole, whole]
        specs += [pl.BlockSpec((feat, wide), lambda j, s: (0, own_block(gate_up_step, s)))] * 2
        specs += [pl.BlockSpec((feat, wide), lambda j, s: (0, oth_block(gate_up_step, s)))] * 2
        shapes.append(jax.ShapeDtypeStruct((rows, 2 * wide), f32))
    operands += [*grad_pair]
    specs += [whole, whole]
    for step in hg_steps:
        operands += [*down_weights]
        specs.append(pl.BlockSpec((wide, feat), lambda j, s, step=step: (own_block(step, s), 0)))
        specs.append(pl.BlockSpec((wide, feat), lambda j, s, step=step: (oth_block(step, s), 0)))
    shapes.append(jax.ShapeDtypeStruct((rows, wide * len(hg_steps)), f32))
    total = sum(shape.shape[1] for shape in shapes)
    shapes.append(jax.ShapeDtypeStruct((rows, total), bf16))
    return pl.pallas_call(
        functools.partial(joint_body, gate_up_step, hg_steps),
        grid_spec=pltpu.PrefetchScalarGridSpec(
            num_scalar_prefetch=1,
            grid=(1,),
            in_specs=specs,
            out_specs=[pl.BlockSpec(shape.shape, lambda j, s: (0, 0)) for shape in shapes],
        ),
        out_shape=shapes,
        compiler_params=params(56),
        cost_estimate=cost(6),
        name="joint_partial",
    )(spot, *operands)


def hidden_body(part_ref, got_ref, hidden_ref, hidden_t_ref):
    gate_up = part_ref[...] + got_ref[...].astype(f32)
    gate_values = gate_up[:, :wide]
    up_values = gate_up[:, wide:]
    silu_values = gate_values * jax.nn.sigmoid(gate_values)
    hidden = (silu_values * up_values).astype(bf16)
    hidden_ref[...] = hidden
    hidden_t_ref[...] = hidden.T


def hidden_step(part, got):
    rows = part.shape[0]
    n = part.shape[1] // (2 * wide)
    pair = pl.BlockSpec((rows, 2 * wide), lambda j: (0, j))
    return pl.pallas_call(
        hidden_body,
        grid=(n,),
        in_specs=[pair, pair],
        out_specs=[
            pl.BlockSpec((rows, wide), lambda j: (0, j)),
            pl.BlockSpec((wide, rows), lambda j: (j, 0)),
        ],
        out_shape=[
            jax.ShapeDtypeStruct((rows, wide * n), bf16),
            jax.ShapeDtypeStruct((wide * n, rows), bf16),
        ],
        compiler_params=params(20),
        cost_estimate=cost(1),
        name="hidden_step",
    )(part, got)


def grads_body(part_ref, got_ref, hg_ref, hg_got_ref, grads_ref):
    gate_up = part_ref[...] + got_ref[...].astype(f32)
    hidden_grad = hg_ref[...] + hg_got_ref[...].astype(f32)
    gate_values = gate_up[:, :wide]
    up_values = gate_up[:, wide:]
    sigmoid_values = jax.nn.sigmoid(gate_values)
    silu_values = gate_values * sigmoid_values
    gate_grad = hidden_grad * up_values * sigmoid_values * (1.0 + gate_values * (1.0 - sigmoid_values))
    up_grad = hidden_grad * silu_values
    grads_ref[:, :wide] = gate_grad.astype(bf16)
    grads_ref[:, wide:] = up_grad.astype(bf16)


def grads_step(hg_at, got_at, part, got, hg, hg_got):
    rows = part.shape[0]
    n = part.shape[1] // (2 * wide)
    pair = pl.BlockSpec((rows, 2 * wide), lambda j: (0, j))
    return pl.pallas_call(
        grads_body,
        grid=(n,),
        in_specs=[
            pair,
            pair,
            pl.BlockSpec((rows, wide), lambda j: (0, hg_at + j)),
            pl.BlockSpec((rows, wide), lambda j: (0, got_at + j)),
        ],
        out_specs=pair,
        out_shape=jax.ShapeDtypeStruct((rows, 2 * wide * n), bf16),
        compiler_params=params(20),
        cost_estimate=cost(1.3),
        name="grads_step",
    )(part, got, hg, hg_got)


def mlp_body(spot, far_ref, near_ref, last_ref, w2, w1, w3, w0, out_ref):
    total = mm(far_ref[...], w2[...]) + mm(near_ref[:, :wide], w1[...])
    total += mm(near_ref[:, wide:], w3[...]) + mm(last_ref[...], w0[...])
    out_ref[...] = total.astype(out_ref.dtype)


def input_body(spot, far_ref, near_ref, last_ref, g2, g1, g3, g0, u2, u1, u3, u0, out_ref):
    total = mm_t(far_ref[:, :wide], g2[...]) + mm_t(far_ref[:, wide:], u2[...])
    total += mm_t(near_ref[:, :wide], g1[...]) + mm_t(near_ref[:, wide : 2 * wide], u1[...])
    total += mm_t(near_ref[:, 2 * wide : 3 * wide], g3[...]) + mm_t(near_ref[:, 3 * wide :], u3[...])
    total += mm_t(last_ref[:, :wide], g0[...]) + mm_t(last_ref[:, wide:], u0[...])
    out_ref[...] = total.astype(out_ref.dtype)


def activation_part(body, block_of, dtype, name, spot, values, weights, by_rows):
    rows = values[0].shape[0]
    feat = weights[0].shape[1 if by_rows else 0]
    whole = [pl.BlockSpec(v.shape, lambda j, s: (0, 0)) for v in values]
    blocks = []
    for _ in weights:
        for step in (2, 1, 3, 0):
            if by_rows:
                blocks.append(pl.BlockSpec((wide, wide), lambda j, s, step=step: (block_of(step, s), j)))
            else:
                blocks.append(pl.BlockSpec((wide, wide), lambda j, s, step=step: (j, block_of(step, s))))
    return pl.pallas_call(
        body,
        grid_spec=pltpu.PrefetchScalarGridSpec(
            num_scalar_prefetch=1,
            grid=(feat // wide,),
            in_specs=whole + blocks,
            out_specs=pl.BlockSpec((rows, wide), lambda j, s: (0, j)),
        ),
        out_shape=jax.ShapeDtypeStruct((rows, feat), dtype),
        compiler_params=params(20),
        cost_estimate=cost(2.5),
        name=name,
    )(spot, *values, *[w for w in weights for _ in range(4)])


def join_body(own_ref, got_ref, out_ref):
    out_ref[...] = (own_ref[...] + got_ref[...].astype(f32)).astype(out_ref.dtype)


def join(dtype, own, got):
    rows, feat = own.shape
    block = pl.BlockSpec((rows // 2, feat), lambda j: (j, 0))
    return pl.pallas_call(
        join_body,
        grid=(2,),
        in_specs=[block, block],
        out_specs=block,
        out_shape=jax.ShapeDtypeStruct(own.shape, dtype),
        compiler_params=params(20),
        cost_estimate=cost(1),
        name="join",
    )(own, got)


def far_body(a0, a1, b0, b1, *out_refs):
    pieces = len(out_refs) // 2
    for a, b, refs in ((a0, b0, out_refs[:pieces]), (a1, b1, out_refs[pieces:])):
        value = mm(a[...], b[...]).astype(bf16)
        n = value.shape[1] // pieces
        for k, ref in enumerate(refs):
            ref[...] = value[:, k * n : (k + 1) * n]


def far_terms(pieces, a, b):
    m, n = a[0].shape[0], b[0].shape[1]
    return pl.pallas_call(
        far_body,
        out_shape=[jax.ShapeDtypeStruct((m, n // pieces), bf16)] * (2 * pieces),
        compiler_params=params(20),
        cost_estimate=cost(1),
        name="far_terms",
    )(*a, *b)


def near_body(a0, a1, c0, c1, b0, b1, d0, d1, *refs):
    pieces = len(refs) // 2 - 1
    rights, lefts = refs[:pieces], refs[pieces : 2 * pieces]
    right_ref, left_ref = refs[-2:]
    m, n = rights[0].shape

    def add(value, got_refs, out_ref, at):
        for k, got in enumerate(got_refs):
            some = value[:, k * n : (k + 1) * n] + got[...].astype(f32)
            out_ref[at : at + m, k * n : (k + 1) * n] = some.astype(bf16)

    add(mm(a0[...], b0[...]), rights, right_ref, 0)
    right_ref[m:, :] = mm(a1[...], b1[...]).astype(bf16)
    left_ref[:m, :] = mm(c0[...], d0[...]).astype(bf16)
    add(mm(c1[...], d1[...]), lefts, left_ref, m)


def window(shape, at):
    return pl.BlockSpec(shape, lambda i: at)


def near_terms(operands, specs, m, n):
    shape = jax.ShapeDtypeStruct((2 * m, n), bf16)
    inner = operands[0].shape[1]
    return pl.pallas_call(
        near_body,
        grid=(1,),
        in_specs=specs,
        out_specs=[window(shape.shape, (0, 0))] * 2,
        out_shape=[shape, shape],
        compiler_params=params(20),
        cost_estimate=cost(2.2),
        name="near_terms",
    )(*operands)


def last_body(spot, a0, a1, b0, b1, from_left, from_right, keep_ref, first_ref, second_ref):
    m = keep_ref.shape[0]
    own = mm(a0[...], b0[...]) + from_left[:m, :].astype(f32) + from_right[:m, :].astype(f32)
    oth = mm(a1[...], b1[...]) + from_left[m:, :].astype(f32) + from_right[m:, :].astype(f32)
    keep_ref[...] = own
    second_ref[...] = oth.astype(bf16)

    @pl.when(spot[3] == 1)
    def _():
        first_ref[...] = oth.astype(bf16)

    @pl.when(spot[3] == 0)
    def _():
        first_ref[...] = own.astype(bf16)


def last_terms(spot, operands, specs, m, n):
    inner = operands[0].shape[1]
    block = pl.BlockSpec((m, n), lambda i, s: (0, 0))
    return pl.pallas_call(
        last_body,
        grid_spec=pltpu.PrefetchScalarGridSpec(
            num_scalar_prefetch=1,
            grid=(1,),
            in_specs=[pl.BlockSpec(shape, lambda i, s, at=at: at) for shape, at in specs],
            out_specs=[block, block, block],
        ),
        out_shape=[
            jax.ShapeDtypeStruct((m, n), f32),
            jax.ShapeDtypeStruct((m, n), bf16),
            jax.ShapeDtypeStruct((m, n), bf16),
        ],
        compiler_params=params(20),
        cost_estimate=cost(1.3),
        name="last_terms",
    )(spot, *operands)


def collect_body(mlp_ref, parts_ref, out_ref):
    height, feat = mlp_ref.shape
    total = parts_ref[:height, :].astype(f32)
    for j in range(1, n_col):
        total = total + parts_ref[j * height : (j + 1) * height, :].astype(f32)
    out_ref[:, :feat] = mlp_ref[...].astype(bf16)
    out_ref[:, feat:] = total.astype(bf16)


def collect(mlp_sum, parts):
    height, feat = mlp_sum.shape
    return pl.pallas_call(
        collect_body,
        out_shape=jax.ShapeDtypeStruct((height, 2 * feat), bf16),
        compiler_params=params(20),
        cost_estimate=cost(1),
        name="collect",
    )(mlp_sum, parts)


def place_body(spot, mine_ref, *refs):
    out_refs = refs[-2:]
    height = mine_ref.shape[0]
    feat = out_refs[0].shape[1]

    def store(step, ref, low):
        at = lax.rem(spot[2] + n_col + step, n_col) * height + low
        for k, out_ref in enumerate(out_refs):
            part = ref[:, k * feat : (k + 1) * feat]
            out_ref[pl.ds(pl.multiple_of(at, ref.shape[0]), ref.shape[0]), :] = part

    store(0, mine_ref, 0)
    for j in range(3):
        store(-1 - j, refs[j], 0)
        store(1 + j, refs[3 + j], 0)
    store(4, refs[6], 0)
    store(4, refs[7], height // 2)


def place(spot, *blocks):
    height, both = blocks[0].shape
    shape = jax.ShapeDtypeStruct((height * n_col, both // 2), bf16)
    return pl.pallas_call(
        place_body,
        grid_spec=pltpu.PrefetchScalarGridSpec(
            num_scalar_prefetch=1,
            grid=(1,),
            in_specs=[pl.BlockSpec(v.shape, lambda j, s: (0, 0)) for v in blocks],
            out_specs=[pl.BlockSpec(shape.shape, lambda j, s: (0, 0))] * 2,
        ),
        out_shape=[shape, shape],
        compiler_params=params(20),
        cost_estimate=cost(1.5),
        name="place",
    )(spot, *blocks)


def finish_body(spot, one_ref, keep_ref, two_ref, *out_refs):
    one = one_ref[...].astype(f32)
    n = out_refs[0].shape[2]

    def store(value):
        for k, out_ref in enumerate(out_refs):
            out_ref[0] = value[:, k * n : (k + 1) * n]

    @pl.when(spot[3] == 1)
    def _():
        store((keep_ref[...] + one) * grad_scale)

    @pl.when(spot[3] == 0)
    def _():
        store((two_ref[...].astype(f32) + one) * grad_scale)


def finish(outs, spot, one, keep, two):
    m, n = one.shape
    block = pl.BlockSpec((m, n), lambda i, s: (0, 0))
    shape = jax.ShapeDtypeStruct((1, m, n // outs), f32)
    return pl.pallas_call(
        finish_body,
        grid_spec=pltpu.PrefetchScalarGridSpec(
            num_scalar_prefetch=1,
            grid=(1,),
            in_specs=[block] * 3,
            out_specs=[pl.BlockSpec(shape.shape, lambda i, s: (0, 0, 0))] * outs,
        ),
        out_shape=[shape] * outs,
        compiler_params=params(20),
        cost_estimate=cost(1.5),
        name="finish",
    )(spot, one, keep, two)


def local(tokens, gate_weight, up_weight, down_weight, output_grad):
    rows, feat = tokens.shape
    depth_id = lax.axis_index("depth")
    x_id = depth_id % n_x
    y_lo = depth_id // n_x
    core = lax.axis_index("row") % 2
    home = core == y_lo
    spot = jnp.stack([x_id, core, lax.axis_index("col"), home.astype(jnp.int32)]).astype(jnp.int32)
    run = Chain()

    swap = lambda value: lax.ppermute(value, "row", core_swap)
    cross = lambda value: lax.ppermute(value, "row", half_swap)
    right = lambda value: lax.ppermute(value, "depth", x_shift(1))
    left = lambda value: lax.ppermute(value, "depth", x_shift(-1))
    home_one = lambda value: lax.ppermute(value, ("depth", "row"), home_first)
    home_two = lambda value: lax.ppermute(value, ("depth", "row"), home_second)
    trade = lambda value: lax.all_to_all(value, "col", 0, 0, tiled=True)

    half = gate_weight.shape[1] // 2
    far, near, last = (2,), (1, 3), (0,)
    oth_columns = lambda value: lax.dynamic_slice_in_dim(value, (1 - core) * half, half, 1)
    oth_rows = lambda value: lax.dynamic_slice_in_dim(value, (1 - core) * half, half, 0)

    tokens_oth = swap(tokens)
    output_grad_oth = swap(output_grad)
    grad_halves = [output_grad, output_grad_oth]
    gate_oth = swap(run(oth_columns, gate_weight))
    up_oth = swap(run(oth_columns, after(up_weight, tokens_oth)))
    gate_up_of = lambda steps: run(
        functools.partial(gate_up_partial, steps),
        spot, tokens, tokens_oth, gate_weight, up_weight, gate_oth, up_oth,
    )
    part_far, send = gate_up_of(far)
    got_far = cross(send)
    down_oth = swap(run(oth_rows, down_weight))
    part_near, send = gate_up_of(near)
    got_near = cross(after(send, got_far))

    hidden_far, hidden_t = run(hidden_step, part_far, got_far)
    down_far = run(lambda a, b0, b1: far_terms(1, (a, a), (b0, b1)), hidden_t, *grad_halves)
    down_far = (right(down_far[0]), left(down_far[1]))
    joint = lambda gate_up_step, hg_steps: run(
        functools.partial(joint_partial, gate_up_step, hg_steps),
        spot,
        (tokens, tokens_oth),
        (gate_weight, up_weight, gate_oth, up_oth),
        grad_halves,
        (down_weight, down_oth),
    )
    part_last, hg_far, send = joint(last[0], far)
    got_last = cross(after(send, got_near))

    hidden_near, hidden_t = run(hidden_step, part_near, got_near)
    t_spec = [window((wide, rows), (0, 0))] * 2 + [window((wide, rows), (1, 0))] * 2
    o_spec = [window((rows, feat), (0, 0))] * 4
    f_spec = [window((wide, feat), (0, 0))] * 2
    down_near = run(
        lambda a, b0, b1, r, l: near_terms(
            (a, a, a, a, b0, b1, b0, b1, r, l), t_spec + o_spec + f_spec, wide, feat
        ),
        hidden_t, *grad_halves, *down_far,
    )
    down_near = (right(down_near[0]), left(down_near[1]))
    hg_rest, send = joint(None, near + last)
    hg_got = cross(after(send, got_last))
    tokens_t = [run(jnp.transpose, value) for value in (tokens, tokens_oth)]

    grads_far = run(functools.partial(grads_step, 0, 2), part_far, got_far, hg_far, got_last)
    gate_up_far = run(lambda b, a0, a1: far_terms(1, (a0, a1), (b, b)), grads_far, *tokens_t)
    gate_up_far = (right(gate_up_far[0]), left(gate_up_far[1]))
    hidden_last, hidden_t = run(hidden_step, part_last, got_last)
    down_spec = (
        [((wide, rows), (0, 0))] * 2 + [((rows, feat), (0, 0))] * 2 + [((2 * wide, feat), (0, 0))] * 2
    )
    down_keep, first, second = run(
        lambda s, a, b0, b1, l, r: last_terms(s, (a, a, b0, b1, l, r), down_spec, wide, feat),
        spot, hidden_t, *grad_halves, *down_near,
    )
    down_first, down_second = home_one(first), home_two(second)
    hidden = (hidden_far, hidden_near, hidden_last)
    mlp_of = lambda block_of, dtype, weight: run(
        lambda s, w, *v: activation_part(mlp_body, block_of, dtype, "mlp_part", s, v, [w], True),
        spot, weight, *hidden,
    )
    mlp_oth = swap(mlp_of(oth_block, bf16, down_oth))
    mlp_own = mlp_of(own_block, f32, down_weight)
    grads_near = run(functools.partial(grads_step, 0, 0), part_near, got_near, hg_rest, hg_got)
    grads_last = run(functools.partial(grads_step, 2, 2), part_last, got_last, hg_rest, hg_got)
    grads = (grads_far, grads_near, grads_last)
    two = 2 * wide
    specs = [window((feat, rows), (0, 0))] * 4
    specs += [window((rows, two), (0, 0))] * 2 + [window((rows, two), (0, 1))] * 2
    specs += [window((feat, two), (0, 0))] * 2
    gate_up_near = run(
        lambda b, a0, a1, *got: near_terms((a0, a1, a0, a1, b, b, b, b, *got), specs, feat, two),
        grads_near, *tokens_t, *gate_up_far,
    )
    gate_up_near = (right(gate_up_near[0]), left(gate_up_near[1]))
    mlp_sum = lax.psum_scatter(
        run(functools.partial(join, f32), mlp_own, mlp_oth), "col", scatter_dimension=0, tiled=True
    )
    input_of = lambda block_of, dtype, *weights: run(
        lambda s, g, u, *v: activation_part(input_body, block_of, dtype, "input_part", s, v, [g, u], False),
        spot, *weights, *grads,
    )
    input_oth = swap(input_of(oth_block, bf16, gate_oth, up_oth))
    input_own = input_of(own_block, f32, gate_weight, up_weight)
    input_parts = trade(run(functools.partial(join, bf16), input_own, input_oth))

    (down_out,) = run(functools.partial(finish, 1), spot, down_first, down_keep, down_second)
    end_spec = [((feat, rows), (0, 0))] * 2 + [((rows, two), (0, 0))] * 2 + [((2 * feat, two), (0, 0))] * 2
    gate_up_keep, first, second = run(
        lambda s, a0, a1, b, l, r: last_terms(s, (a0, a1, b, b, l, r), end_spec, feat, two),
        spot, *tokens_t, grads_last, *gate_up_near,
    )
    gate_up_first, gate_up_second = home_one(first), home_two(second)
    both = run(collect, mlp_sum, input_parts)
    col_right = lambda value: lax.ppermute(value, "col", [(i, (i + 1) % n_col) for i in range(n_col)])
    col_left = lambda value: lax.ppermute(value, "col", [(i, (i - 1) % n_col) for i in range(n_col)])
    from_left, from_right = [col_right(both)], [col_left(both)]
    for _ in range(2):
        from_left.append(col_right(from_left[-1]))
        from_right.append(col_left(from_right[-1]))
    quarter = both.shape[0] // 2
    end_left = col_right(from_left[-1][:quarter])
    end_right = col_left(from_right[-1][quarter:])
    gate_out, up_out = run(functools.partial(finish, 2), spot, gate_up_first, gate_up_keep, gate_up_second)
    mlp_output, input_grad = run(place, spot, both, *from_left, *from_right, end_left, end_right)
    return (mlp_output, input_grad, gate_out, up_out, down_out)


def solution(mesh):
    placed = (
        P("depth", "row"),
        P("row", "col"),
        P("row", "col"),
        P("col", "row"),
        P("depth", "row"),
    )
    return jax.shard_map(
        local,
        mesh=mesh,
        in_specs=placed,
        out_specs=(
            P("depth", "row"),
            P("depth", "row"),
            P("depth", "row", "col"),
            P("depth", "row", "col"),
            P("depth", "col", "row"),
        ),
        check_vma=False,
    )
```

```python
import functools

import jax
import jax.numpy as jnp
from jax import lax
from jax.experimental import pallas as pl
from jax.experimental.pallas import tpu as pltpu
from jax.sharding import PartitionSpec as P

grad_scale = 0.03125
wide = 256
n_x = 4
n_col = 8
mib = 1024 * 1024
bf16 = jnp.bfloat16
f32 = jnp.float32

core_swap = [(0, 1), (1, 0), (2, 3), (3, 2)]
half_swap = [(0, 2), (2, 0), (1, 3), (3, 1)]


def x_shift(step):
    return [(y * n_x + x, y * n_x + (x + step) % n_x) for y in range(2) for x in range(n_x)]


def home_swaps():
    first, second = [], []
    for y in range(2):
        for x in range(n_x):
            for half in range(2):
                for core in range(2):
                    at = lambda y_to, core_to: (y_to * n_x + x) * 4 + half * 2 + core_to
                    if core == y:
                        first.append((at(y, core), at(y, 1 - core)))
                    else:
                        first.append((at(y, core), at(1 - y, core)))
                        second.append((at(y, core), at(1 - y, 1 - core)))
    return first, second


home_first, home_second = home_swaps()


def params(limit):
    return pltpu.CompilerParams(vmem_limit_bytes=limit * mib)


def cost(time):
    return pl.CostEstimate(flops=1, bytes_accessed=int(time * 1 * 3.3e6), transcendentals=0)


def mm(left, right):
    return jnp.dot(left, right, preferred_element_type=f32)


def mm_t(left, right):
    return lax.dot_general(left, right, (((1,), (1,)), ((), ())), preferred_element_type=f32)


def after(value, *others):
    return lax.optimization_barrier((value,) + others)[0]


class Chain:
    def __init__(self):
        self.last = None

    def __call__(self, fn, *args):
        if self.last is not None:
            args = (after(args[0], self.last),) + args[1:]
        out = fn(*args)
        self.last = out[0] if isinstance(out, (tuple, list)) else out
        return out


def own_block(step, spot):
    return spot[1] * n_x + lax.rem(spot[0] + step, n_x)


def oth_block(step, spot):
    return lax.rem(spot[0] + step, n_x)


def gate_up_body(spot, own_ref, oth_ref, gate_ref, up_ref, oth_gate_ref, oth_up_ref, out_ref, send_ref):
    for k, (w, oth_w) in enumerate(((gate_ref, oth_gate_ref), (up_ref, oth_up_ref))):
        value = mm(own_ref[...], w[...]) + mm(oth_ref[...], oth_w[...])
        out_ref[:, k * wide : (k + 1) * wide] = value
        send_ref[:, k * wide : (k + 1) * wide] = value.astype(bf16)


def gate_up_partial(steps, spot, own, oth, gate_weight, up_weight, oth_gate, oth_up):
    rows, feat = own.shape
    n = len(steps)
    part = pl.BlockSpec((rows // 2, feat), lambda j, i, s: (i, 0))
    own_w = pl.BlockSpec((feat, wide), lambda j, i, s: (0, own_block(steps[0] + 2 * j, s)))
    oth_w = pl.BlockSpec((feat, wide), lambda j, i, s: (0, oth_block(steps[0] + 2 * j, s)))
    out = pl.BlockSpec((rows // 2, 2 * wide), lambda j, i, s: (i, j))
    return pl.pallas_call(
        gate_up_body,
        grid_spec=pltpu.PrefetchScalarGridSpec(
            num_scalar_prefetch=1,
            grid=(n, 2),
            in_specs=[part, part, own_w, own_w, oth_w, oth_w],
            out_specs=[out, out],
        ),
        out_shape=[
            jax.ShapeDtypeStruct((rows, 2 * wide * n), f32),
            jax.ShapeDtypeStruct((rows, 2 * wide * n), bf16),
        ],
        compiler_params=params(56),
        cost_estimate=cost(4.5),
        name="gate_up_partial",
    )(spot, own, oth, gate_weight, up_weight, oth_gate, oth_up)


def joint_body(gate_up_step, hg_steps, spot, *refs):
    refs = list(refs)
    send_ref, outs = refs[-1], []
    at = 0
    if gate_up_step is not None:
        own_ref, oth_ref, gate_ref, up_ref, oth_gate_ref, oth_up_ref = refs[:6]
        refs = refs[6:]
        out_ref = refs[-2] if not hg_steps else refs[-3]
        for k, (w, oth_w) in enumerate(((gate_ref, oth_gate_ref), (up_ref, oth_up_ref))):
            value = mm(own_ref[...], w[...]) + mm(oth_ref[...], oth_w[...])
            out_ref[:, k * wide : (k + 1) * wide] = value
            send_ref[:, k * wide : (k + 1) * wide] = value.astype(bf16)
        at = 2 * wide
    own_ref, oth_ref = refs[:2]
    out_ref = refs[-2]
    for k in range(len(hg_steps)):
        value = mm_t(own_ref[...], refs[2 + 2 * k][...]) + mm_t(oth_ref[...], refs[3 + 2 * k][...])
        out_ref[:, k * wide : (k + 1) * wide] = value
        send_ref[:, at + k * wide : at + (k + 1) * wide] = value.astype(bf16)


def joint_partial(gate_up_step, hg_steps, spot, tokens_pair, gate_up_weights, grad_pair, down_weights):
    rows, feat = grad_pair[0].shape
    whole = pl.BlockSpec((rows, feat), lambda j, s: (0, 0))
    operands, specs, shapes = [], [], []
    if gate_up_step is not None:
        operands += [*tokens_pair, *gate_up_weights]
        specs += [whole, whole]
        specs += [pl.BlockSpec((feat, wide), lambda j, s: (0, own_block(gate_up_step, s)))] * 2
        specs += [pl.BlockSpec((feat, wide), lambda j, s: (0, oth_block(gate_up_step, s)))] * 2
        shapes.append(jax.ShapeDtypeStruct((rows, 2 * wide), f32))
    operands += [*grad_pair]
    specs += [whole, whole]
    for step in hg_steps:
        operands += [*down_weights]
        specs.append(pl.BlockSpec((wide, feat), lambda j, s, step=step: (own_block(step, s), 0)))
        specs.append(pl.BlockSpec((wide, feat), lambda j, s, step=step: (oth_block(step, s), 0)))
    shapes.append(jax.ShapeDtypeStruct((rows, wide * len(hg_steps)), f32))
    total = sum(shape.shape[1] for shape in shapes)
    shapes.append(jax.ShapeDtypeStruct((rows, total), bf16))
    return pl.pallas_call(
        functools.partial(joint_body, gate_up_step, hg_steps),
        grid_spec=pltpu.PrefetchScalarGridSpec(
            num_scalar_prefetch=1,
            grid=(1,),
            in_specs=specs,
            out_specs=[pl.BlockSpec(shape.shape, lambda j, s: (0, 0)) for shape in shapes],
        ),
        out_shape=shapes,
        compiler_params=params(56),
        cost_estimate=cost(6),
        name="joint_partial",
    )(spot, *operands)


def hidden_body(part_ref, got_ref, hidden_ref, hidden_t_ref):
    gate_up = part_ref[...] + got_ref[...].astype(f32)
    gate_values = gate_up[:, :wide]
    up_values = gate_up[:, wide:]
    silu_values = gate_values * jax.nn.sigmoid(gate_values)
    hidden = (silu_values * up_values).astype(bf16)
    hidden_ref[...] = hidden
    hidden_t_ref[...] = hidden.T


def hidden_step(part, got):
    rows = part.shape[0]
    n = part.shape[1] // (2 * wide)
    pair = pl.BlockSpec((rows, 2 * wide), lambda j: (0, j))
    return pl.pallas_call(
        hidden_body,
        grid=(n,),
        in_specs=[pair, pair],
        out_specs=[
            pl.BlockSpec((rows, wide), lambda j: (0, j)),
            pl.BlockSpec((wide, rows), lambda j: (j, 0)),
        ],
        out_shape=[
            jax.ShapeDtypeStruct((rows, wide * n), bf16),
            jax.ShapeDtypeStruct((wide * n, rows), bf16),
        ],
        compiler_params=params(20),
        cost_estimate=cost(1),
        name="hidden_step",
    )(part, got)


def grads_body(part_ref, got_ref, hg_ref, hg_got_ref, grads_ref):
    gate_up = part_ref[...] + got_ref[...].astype(f32)
    hidden_grad = hg_ref[...] + hg_got_ref[...].astype(f32)
    gate_values = gate_up[:, :wide]
    up_values = gate_up[:, wide:]
    sigmoid_values = jax.nn.sigmoid(gate_values)
    silu_values = gate_values * sigmoid_values
    gate_grad = hidden_grad * up_values * sigmoid_values * (1.0 + gate_values * (1.0 - sigmoid_values))
    up_grad = hidden_grad * silu_values
    grads_ref[:, :wide] = gate_grad.astype(bf16)
    grads_ref[:, wide:] = up_grad.astype(bf16)


def grads_step(hg_at, got_at, part, got, hg, hg_got):
    rows = part.shape[0]
    n = part.shape[1] // (2 * wide)
    pair = pl.BlockSpec((rows, 2 * wide), lambda j: (0, j))
    return pl.pallas_call(
        grads_body,
        grid=(n,),
        in_specs=[
            pair,
            pair,
            pl.BlockSpec((rows, wide), lambda j: (0, hg_at + j)),
            pl.BlockSpec((rows, wide), lambda j: (0, got_at + j)),
        ],
        out_specs=pair,
        out_shape=jax.ShapeDtypeStruct((rows, 2 * wide * n), bf16),
        compiler_params=params(20),
        cost_estimate=cost(1.3),
        name="grads_step",
    )(part, got, hg, hg_got)


def mlp_body(spot, far_ref, near_ref, last_ref, w2, w1, w3, w0, out_ref):
    total = mm(far_ref[...], w2[...]) + mm(near_ref[:, :wide], w1[...])
    total += mm(near_ref[:, wide:], w3[...]) + mm(last_ref[...], w0[...])
    out_ref[...] = total.astype(out_ref.dtype)


def input_body(spot, far_ref, near_ref, last_ref, g2, g1, g3, g0, u2, u1, u3, u0, out_ref):
    total = mm_t(far_ref[:, :wide], g2[...]) + mm_t(far_ref[:, wide:], u2[...])
    total += mm_t(near_ref[:, :wide], g1[...]) + mm_t(near_ref[:, wide : 2 * wide], u1[...])
    total += mm_t(near_ref[:, 2 * wide : 3 * wide], g3[...]) + mm_t(near_ref[:, 3 * wide :], u3[...])
    total += mm_t(last_ref[:, :wide], g0[...]) + mm_t(last_ref[:, wide:], u0[...])
    out_ref[...] = total.astype(out_ref.dtype)


def activation_part(body, block_of, dtype, name, spot, values, weights, by_rows):
    rows = values[0].shape[0]
    feat = weights[0].shape[1 if by_rows else 0]
    whole = [pl.BlockSpec(v.shape, lambda j, s: (0, 0)) for v in values]
    blocks = []
    for _ in weights:
        for step in (2, 1, 3, 0):
            if by_rows:
                blocks.append(pl.BlockSpec((wide, wide), lambda j, s, step=step: (block_of(step, s), j)))
            else:
                blocks.append(pl.BlockSpec((wide, wide), lambda j, s, step=step: (j, block_of(step, s))))
    return pl.pallas_call(
        body,
        grid_spec=pltpu.PrefetchScalarGridSpec(
            num_scalar_prefetch=1,
            grid=(feat // wide,),
            in_specs=whole + blocks,
            out_specs=pl.BlockSpec((rows, wide), lambda j, s: (0, j)),
        ),
        out_shape=jax.ShapeDtypeStruct((rows, feat), dtype),
        compiler_params=params(20),
        cost_estimate=cost(2.5),
        name=name,
    )(spot, *values, *[w for w in weights for _ in range(4)])


def join_body(own_ref, got_ref, out_ref):
    out_ref[...] = (own_ref[...] + got_ref[...].astype(f32)).astype(out_ref.dtype)


def join(dtype, own, got):
    rows, feat = own.shape
    block = pl.BlockSpec((rows // 2, feat), lambda j: (j, 0))
    return pl.pallas_call(
        join_body,
        grid=(2,),
        in_specs=[block, block],
        out_specs=block,
        out_shape=jax.ShapeDtypeStruct(own.shape, dtype),
        compiler_params=params(20),
        cost_estimate=cost(1),
        name="join",
    )(own, got)


def far_body(a0, a1, b0, b1, *out_refs):
    pieces = len(out_refs) // 2
    for a, b, refs in ((a0, b0, out_refs[:pieces]), (a1, b1, out_refs[pieces:])):
        value = mm(a[...], b[...]).astype(bf16)
        n = value.shape[1] // pieces
        for k, ref in enumerate(refs):
            ref[...] = value[:, k * n : (k + 1) * n]


def far_terms(pieces, a, b):
    m, n = a[0].shape[0], b[0].shape[1]
    return pl.pallas_call(
        far_body,
        out_shape=[jax.ShapeDtypeStruct((m, n // pieces), bf16)] * (2 * pieces),
        compiler_params=params(20),
        cost_estimate=cost(1),
        name="far_terms",
    )(*a, *b)


def near_body(a0, a1, c0, c1, b0, b1, d0, d1, *refs):
    pieces = len(refs) // 2 - 1
    rights, lefts = refs[:pieces], refs[pieces : 2 * pieces]
    right_ref, left_ref = refs[-2:]
    m, n = rights[0].shape

    def add(value, got_refs, out_ref, at):
        for k, got in enumerate(got_refs):
            some = value[:, k * n : (k + 1) * n] + got[...].astype(f32)
            out_ref[at : at + m, k * n : (k + 1) * n] = some.astype(bf16)

    add(mm(a0[...], b0[...]), rights, right_ref, 0)
    right_ref[m:, :] = mm(a1[...], b1[...]).astype(bf16)
    left_ref[:m, :] = mm(c0[...], d0[...]).astype(bf16)
    add(mm(c1[...], d1[...]), lefts, left_ref, m)


def window(shape, at):
    return pl.BlockSpec(shape, lambda i: at)


def near_terms(operands, specs, m, n):
    shape = jax.ShapeDtypeStruct((2 * m, n), bf16)
    inner = operands[0].shape[1]
    return pl.pallas_call(
        near_body,
        grid=(1,),
        in_specs=specs,
        out_specs=[window(shape.shape, (0, 0))] * 2,
        out_shape=[shape, shape],
        compiler_params=params(20),
        cost_estimate=cost(2.2),
        name="near_terms",
    )(*operands)


def last_body(spot, a0, a1, b0, b1, from_left, from_right, keep_ref, first_ref, second_ref):
    m = keep_ref.shape[0]
    own = mm(a0[...], b0[...]) + from_left[:m, :].astype(f32) + from_right[:m, :].astype(f32)
    oth = mm(a1[...], b1[...]) + from_left[m:, :].astype(f32) + from_right[m:, :].astype(f32)
    keep_ref[...] = own
    second_ref[...] = oth.astype(bf16)

    @pl.when(spot[3] == 1)
    def _():
        first_ref[...] = oth.astype(bf16)

    @pl.when(spot[3] == 0)
    def _():
        first_ref[...] = own.astype(bf16)


def last_terms(spot, operands, specs, m, n):
    inner = operands[0].shape[1]
    block = pl.BlockSpec((m, n), lambda i, s: (0, 0))
    return pl.pallas_call(
        last_body,
        grid_spec=pltpu.PrefetchScalarGridSpec(
            num_scalar_prefetch=1,
            grid=(1,),
            in_specs=[pl.BlockSpec(shape, lambda i, s, at=at: at) for shape, at in specs],
            out_specs=[block, block, block],
        ),
        out_shape=[
            jax.ShapeDtypeStruct((m, n), f32),
            jax.ShapeDtypeStruct((m, n), bf16),
            jax.ShapeDtypeStruct((m, n), bf16),
        ],
        compiler_params=params(20),
        cost_estimate=cost(1.3),
        name="last_terms",
    )(spot, *operands)


def collect_body(*refs):
    out_ref = refs[-1]
    height = out_ref.shape[0]
    for k, parts_ref in enumerate(refs[:-1]):
        feat = parts_ref.shape[1]
        total = parts_ref[:height, :].astype(f32)
        for j in range(1, n_col):
            total = total + parts_ref[j * height : (j + 1) * height, :].astype(f32)
        out_ref[:, k * feat : (k + 1) * feat] = total.astype(bf16)


def collect(*parts):
    rows, feat = parts[0].shape
    return pl.pallas_call(
        collect_body,
        out_shape=jax.ShapeDtypeStruct((rows // n_col, len(parts) * feat), bf16),
        compiler_params=params(20),
        cost_estimate=cost(1),
        name="collect",
    )(*parts)


def place_body(spot, mine_ref, *refs):
    out_refs = refs[-2:]
    height = mine_ref.shape[0]
    feat = out_refs[0].shape[1]

    def store(step, ref, low):
        at = lax.rem(spot[2] + n_col + step, n_col) * height + low
        for k, out_ref in enumerate(out_refs):
            part = ref[:, k * feat : (k + 1) * feat]
            out_ref[pl.ds(pl.multiple_of(at, ref.shape[0]), ref.shape[0]), :] = part

    store(0, mine_ref, 0)
    for j in range(3):
        store(-1 - j, refs[j], 0)
        store(1 + j, refs[3 + j], 0)
    store(4, refs[6], 0)
    store(4, refs[7], height // 2)


def place(spot, *blocks):
    height, both = blocks[0].shape
    shape = jax.ShapeDtypeStruct((height * n_col, both // 2), bf16)
    return pl.pallas_call(
        place_body,
        grid_spec=pltpu.PrefetchScalarGridSpec(
            num_scalar_prefetch=1,
            grid=(1,),
            in_specs=[pl.BlockSpec(v.shape, lambda j, s: (0, 0)) for v in blocks],
            out_specs=[pl.BlockSpec(shape.shape, lambda j, s: (0, 0))] * 2,
        ),
        out_shape=[shape, shape],
        compiler_params=params(20),
        cost_estimate=cost(1.5),
        name="place",
    )(spot, *blocks)


def finish_body(spot, one_ref, keep_ref, two_ref, *out_refs):
    one = one_ref[...].astype(f32)
    n = out_refs[0].shape[2]

    def store(value):
        for k, out_ref in enumerate(out_refs):
            out_ref[0] = value[:, k * n : (k + 1) * n]

    @pl.when(spot[3] == 1)
    def _():
        store((keep_ref[...] + one) * grad_scale)

    @pl.when(spot[3] == 0)
    def _():
        store((two_ref[...].astype(f32) + one) * grad_scale)


def finish(outs, spot, one, keep, two):
    m, n = one.shape
    block = pl.BlockSpec((m, n), lambda i, s: (0, 0))
    shape = jax.ShapeDtypeStruct((1, m, n // outs), f32)
    return pl.pallas_call(
        finish_body,
        grid_spec=pltpu.PrefetchScalarGridSpec(
            num_scalar_prefetch=1,
            grid=(1,),
            in_specs=[block] * 3,
            out_specs=[pl.BlockSpec(shape.shape, lambda i, s: (0, 0, 0))] * outs,
        ),
        out_shape=[shape] * outs,
        compiler_params=params(20),
        cost_estimate=cost(1.5),
        name="finish",
    )(spot, one, keep, two)


def local(tokens, gate_weight, up_weight, down_weight, output_grad):
    rows, feat = tokens.shape
    depth_id = lax.axis_index("depth")
    x_id = depth_id % n_x
    y_lo = depth_id // n_x
    core = lax.axis_index("row") % 2
    home = core == y_lo
    spot = jnp.stack([x_id, core, lax.axis_index("col"), home.astype(jnp.int32)]).astype(jnp.int32)
    run = Chain()

    swap = lambda value: lax.ppermute(value, "row", core_swap)
    cross = lambda value: lax.ppermute(value, "row", half_swap)
    right = lambda value: lax.ppermute(value, "depth", x_shift(1))
    left = lambda value: lax.ppermute(value, "depth", x_shift(-1))
    home_one = lambda value: lax.ppermute(value, ("depth", "row"), home_first)
    home_two = lambda value: lax.ppermute(value, ("depth", "row"), home_second)
    trade = lambda value: lax.all_to_all(value, "col", 0, 0, tiled=True)

    half = gate_weight.shape[1] // 2
    far, near, last = (2,), (1, 3), (0,)
    oth_columns = lambda value: lax.dynamic_slice_in_dim(value, (1 - core) * half, half, 1)
    oth_rows = lambda value: lax.dynamic_slice_in_dim(value, (1 - core) * half, half, 0)

    tokens_oth = swap(tokens)
    output_grad_oth = swap(output_grad)
    grad_halves = [output_grad, output_grad_oth]
    gate_oth = swap(run(oth_columns, gate_weight))
    up_oth = swap(run(oth_columns, after(up_weight, tokens_oth)))
    gate_up_of = lambda steps: run(
        functools.partial(gate_up_partial, steps),
        spot, tokens, tokens_oth, gate_weight, up_weight, gate_oth, up_oth,
    )
    part_far, send = gate_up_of(far)
    got_far = cross(send)
    down_oth = swap(run(oth_rows, down_weight))
    part_near, send = gate_up_of(near)
    got_near = cross(after(send, got_far))

    hidden_far, hidden_t = run(hidden_step, part_far, got_far)
    down_far = run(lambda a, b0, b1: far_terms(1, (a, a), (b0, b1)), hidden_t, *grad_halves)
    down_far = (right(down_far[0]), left(down_far[1]))
    joint = lambda gate_up_step, hg_steps: run(
        functools.partial(joint_partial, gate_up_step, hg_steps),
        spot,
        (tokens, tokens_oth),
        (gate_weight, up_weight, gate_oth, up_oth),
        grad_halves,
        (down_weight, down_oth),
    )
    part_last, hg_far, send = joint(last[0], far)
    got_last = cross(after(send, got_near))

    hidden_near, hidden_t = run(hidden_step, part_near, got_near)
    t_spec = [window((wide, rows), (0, 0))] * 2 + [window((wide, rows), (1, 0))] * 2
    o_spec = [window((rows, feat), (0, 0))] * 4
    f_spec = [window((wide, feat), (0, 0))] * 2
    down_near = run(
        lambda a, b0, b1, r, l: near_terms(
            (a, a, a, a, b0, b1, b0, b1, r, l), t_spec + o_spec + f_spec, wide, feat
        ),
        hidden_t, *grad_halves, *down_far,
    )
    down_near = (right(down_near[0]), left(down_near[1]))
    hg_rest, send = joint(None, near + last)
    hg_got = cross(after(send, got_last))
    tokens_t = [run(jnp.transpose, value) for value in (tokens, tokens_oth)]

    grads_far = run(functools.partial(grads_step, 0, 2), part_far, got_far, hg_far, got_last)
    gate_up_far = run(lambda b, a0, a1: far_terms(1, (a0, a1), (b, b)), grads_far, *tokens_t)
    gate_up_far = (right(gate_up_far[0]), left(gate_up_far[1]))
    hidden_last, hidden_t = run(hidden_step, part_last, got_last)
    down_spec = (
        [((wide, rows), (0, 0))] * 2 + [((rows, feat), (0, 0))] * 2 + [((2 * wide, feat), (0, 0))] * 2
    )
    down_keep, first, second = run(
        lambda s, a, b0, b1, l, r: last_terms(s, (a, a, b0, b1, l, r), down_spec, wide, feat),
        spot, hidden_t, *grad_halves, *down_near,
    )
    down_first, down_second = home_one(first), home_two(second)
    hidden = (hidden_far, hidden_near, hidden_last)
    mlp_of = lambda block_of, dtype, weight: run(
        lambda s, w, *v: activation_part(mlp_body, block_of, dtype, "mlp_part", s, v, [w], True),
        spot, weight, *hidden,
    )
    mlp_oth = swap(mlp_of(oth_block, bf16, down_oth))
    mlp_own = mlp_of(own_block, f32, down_weight)
    grads_near = run(functools.partial(grads_step, 0, 0), part_near, got_near, hg_rest, hg_got)
    grads_last = run(functools.partial(grads_step, 2, 2), part_last, got_last, hg_rest, hg_got)
    grads = (grads_far, grads_near, grads_last)
    two = 2 * wide
    specs = [window((feat, rows), (0, 0))] * 4
    specs += [window((rows, two), (0, 0))] * 2 + [window((rows, two), (0, 1))] * 2
    specs += [window((feat, two), (0, 0))] * 2
    gate_up_near = run(
        lambda b, a0, a1, *got: near_terms((a0, a1, a0, a1, b, b, b, b, *got), specs, feat, two),
        grads_near, *tokens_t, *gate_up_far,
    )
    gate_up_near = (right(gate_up_near[0]), left(gate_up_near[1]))
    mlp_parts = trade(run(functools.partial(join, bf16), mlp_own, mlp_oth))
    input_of = lambda block_of, dtype, *weights: run(
        lambda s, g, u, *v: activation_part(input_body, block_of, dtype, "input_part", s, v, [g, u], False),
        spot, *weights, *grads,
    )
    input_oth = swap(input_of(oth_block, bf16, gate_oth, up_oth))
    input_own = input_of(own_block, f32, gate_weight, up_weight)
    input_parts = trade(run(functools.partial(join, bf16), input_own, input_oth))

    (down_out,) = run(functools.partial(finish, 1), spot, down_first, down_keep, down_second)
    end_spec = [((feat, rows), (0, 0))] * 2 + [((rows, two), (0, 0))] * 2 + [((2 * feat, two), (0, 0))] * 2
    gate_up_keep, first, second = run(
        lambda s, a0, a1, b, l, r: last_terms(s, (a0, a1, b, b, l, r), end_spec, feat, two),
        spot, *tokens_t, grads_last, *gate_up_near,
    )
    gate_up_first, gate_up_second = home_one(first), home_two(second)
    both = run(collect, mlp_parts, input_parts)
    col_right = lambda value: lax.ppermute(value, "col", [(i, (i + 1) % n_col) for i in range(n_col)])
    col_left = lambda value: lax.ppermute(value, "col", [(i, (i - 1) % n_col) for i in range(n_col)])
    from_left, from_right = [col_right(both)], [col_left(both)]
    for _ in range(2):
        from_left.append(col_right(from_left[-1]))
        from_right.append(col_left(from_right[-1]))
    quarter = both.shape[0] // 2
    end_left = col_right(from_left[-1][:quarter])
    end_right = col_left(from_right[-1][quarter:])
    gate_out, up_out = run(functools.partial(finish, 2), spot, gate_up_first, gate_up_keep, gate_up_second)
    mlp_output, input_grad = run(place, spot, both, *from_left, *from_right, end_left, end_right)
    return (mlp_output, input_grad, gate_out, up_out, down_out)


def solution(mesh):
    placed = (
        P("depth", "row"),
        P("row", "col"),
        P("row", "col"),
        P("col", "row"),
        P("depth", "row"),
    )
    return jax.shard_map(
        local,
        mesh=mesh,
        in_specs=placed,
        out_specs=(
            P("depth", "row"),
            P("depth", "row"),
            P("depth", "row", "col"),
            P("depth", "row", "col"),
            P("depth", "col", "row"),
        ),
        check_vma=False,
    )
```
